256 devices in a mesh: seq: 32 (over z, y), tensor: 8 (over x, core).
Axes of the slice: x: 4, y: 4, z: 8, core: 2. Of those that a mesh axis runs over, the one named last changes fastest.
Arguments:
- queries: bfloat16 [32768, 4096], P('seq', 'tensor'), may hold values from -6 to 6
- cotangent: bfloat16 [32768, 4096], P('seq', 'tensor'), may hold values from -6 to 6
- neighbours: bfloat16 [256, 128, 896], P('seq'), may hold values from -6 to 6
- key_weight: bfloat16 [896, 4096], P(None, 'tensor'), may hold values from -0.1875 to 0.1875
- value_weight: bfloat16 [896, 4096], P(None, 'tensor'), may hold values from -0.1875 to 0.1875
- retrieval: int32 [512, 2], P('seq'), may hold values from 0 to 255, as said below
Outputs:
- attended: bfloat16 [32768, 4096], P('seq', 'tensor')
- query_grad: bfloat16 [32768, 4096], P('seq', 'tensor')
- neighbour_grad: bfloat16 [256, 128, 896], P('seq', None, 'tensor')
The draws below stay inside these ranges and needn't reach their ends.
Inputs may be any that keep to these rules, and one draw needn't show every extreme that they name: `retrieval`: entry e is held by index e // 8 of seq. Each row names two different entries of one holder. Of the 16 rows of one device, at most 2 name entries of the same holder, and in every draw one holder is named by exactly 2 rows of every device.
All inputs are finite; a program needn't handle non-finite values.
Results may differ from the reference program's by a relative error of at most 0.019.
Values may be sent and summed in bfloat16 or wider, within the bound.
No kernel may reach another device: no remote copies, remote signals or barrier semaphores. Data moves between devices by JAX's collectives and lax.ppermute only.
A program may use at most 192 MiB of HBM per device.

```python
import math
import jax
import jax.numpy as jnp
from jax import lax

D = 4096
HEADS = 32
ENC = 896
HEAD_DIM = 128
BLOCK_LEN = 64
NBR_LEN = 128
SEQ_LEN = 2048
BLOCKS_DEV = 16
CAP = 2
ENT_DEV = 8
TOKENS = 32768
BLOCKS = 512
ENTRIES = 256


def draw_retrieval(key, part):
    key = jax.random.fold_in(key, 11)
    holders = BLOCKS // BLOCKS_DEV
    hot_key, block_key = jax.random.split(key)
    hot_holder = jax.random.randint(hot_key, (), 0, holders)

    def one_device(device_key):
        first_key, second_key, third_key, fourth_key = jax.random.split(device_key, 4)
        picked = jax.random.permutation(first_key, (holders - 1) * CAP)[:BLOCKS_DEV - CAP] // CAP
        picked = picked.astype(jnp.int32)
        picked = picked + (picked >= hot_holder).astype(jnp.int32)
        holder_rows = jnp.concatenate([jnp.full((CAP,), hot_holder, jnp.int32), picked])
        holder_rows = holder_rows[jax.random.permutation(second_key, BLOCKS_DEV)]
        first_entry = jax.random.randint(third_key, (BLOCKS_DEV,), 0, ENT_DEV)
        stride = jax.random.randint(fourth_key, (BLOCKS_DEV,), 1, ENT_DEV)
        second_entry = (first_entry + stride) % ENT_DEV
        return jnp.stack([holder_rows * ENT_DEV + first_entry, holder_rows * ENT_DEV + second_entry], axis=1)
    table = jax.vmap(one_device)(jax.random.split(block_key, holders))
    return table.reshape(BLOCKS, 2).astype(jnp.int32)


def block_levels(rng, shape, cuts, least, largest):
    loudness, own = 1.0, jax.random.fold_in(rng, 6)
    for dim, parts in cuts:
        draws = jnp.exp(jax.random.uniform(jax.random.fold_in(own, dim), (parts,), jnp.float32, least / len(cuts), largest / len(cuts)))
        loudness = loudness * jnp.repeat(draws, shape[dim] // parts).reshape([-1 if axis == dim else 1 for axis in range(len(shape))])
    return loudness


def centred(own_key, shape, scale, reach, cuts=(), kind=jnp.bfloat16):
    array = scale * jax.random.normal(own_key, shape, jnp.float32)
    if cuts:
        array = array * block_levels(own_key, shape, cuts, -0.22, 0.18)
    return jnp.clip(array, -reach, reach).astype(kind)


def setup_inputs(seed: int = 0) -> dict:
    key_of = jax.random.split(jax.random.key(seed), 7)
    return {
        "queries": centred(key_of[0], (TOKENS, D), 1.0, 6.0, ((0, 32), (1, 8))),
        "cotangent": centred(key_of[1], (TOKENS, D), 1.0, 6.0, ((0, 32), (1, 8))),
        "neighbours": centred(key_of[2], (ENTRIES, NBR_LEN, ENC), 1.0, 6.0, ((0, 32),)),
        "key_weight": centred(key_of[3], (ENC, D), ENC ** -0.5, 0.1875, ((1, 8),)),
        "value_weight": centred(key_of[4], (ENC, D), ENC ** -0.5, 0.1875, ((1, 8),)),
        "retrieval": draw_retrieval(jax.random.fold_in(key_of[6], 71), 0),
    }


def grouped(source_rows, sequence_count, offset_rows, group_count):
    shaped = source_rows.reshape(sequence_count, SEQ_LEN, D)
    padding = jnp.zeros((sequence_count, offset_rows, D), shaped.dtype)
    moved_up = jnp.concatenate([shaped[:, offset_rows:], padding], axis=1)
    return moved_up.reshape(group_count, -1, BLOCK_LEN, D)

def ungrouped(group_rows, sequence_count, offset_rows):
    shaped = group_rows.reshape(sequence_count, SEQ_LEN, D)
    padding = jnp.zeros((sequence_count, offset_rows, D), shaped.dtype)
    moved_down = jnp.concatenate([padding, shaped[:, :SEQ_LEN - offset_rows]], axis=1)
    return moved_down.reshape(TOKENS, D)

def project(neighbours, weight):
    flattened = neighbours.reshape(ENTRIES * NBR_LEN, ENC)
    product = jnp.dot(flattened, weight, preferred_element_type=jnp.float32)
    return product.astype(jnp.bfloat16).reshape(ENTRIES, NBR_LEN, D)

def reference(queries, cotangent, neighbours, key_weight, value_weight, retrieval):
    offset_rows = BLOCK_LEN - 1
    sequence_count = TOKENS // SEQ_LEN
    group_size = math.gcd(BLOCKS, 16)
    group_count = BLOCKS // group_size
    score_scale = 1.0 / math.sqrt(HEAD_DIM)
    highest = lax.Precision.HIGHEST
    key_rows = project(neighbours, key_weight)
    value_rows = project(neighbours, value_weight)
    query_groups = grouped(queries, sequence_count, offset_rows, group_count)
    grad_groups = grouped(cotangent, sequence_count, offset_rows, group_count)
    pair_groups = retrieval.reshape(group_count, group_size, 2).astype(jnp.int32)

    def step(totals, pieces):
        query_block, grad_block, entry_pair = pieces
        flat_pair = entry_pair.reshape(-1)
        key_float = key_rows[flat_pair].reshape(group_size, 2 * NBR_LEN, HEADS, HEAD_DIM).astype(jnp.float32)
        value_float = value_rows[flat_pair].reshape(group_size, 2 * NBR_LEN, HEADS, HEAD_DIM).astype(jnp.float32)
        query_heads = query_block.reshape(group_size, BLOCK_LEN, HEADS, HEAD_DIM).astype(jnp.float32)
        grad_heads = grad_block.reshape(group_size, BLOCK_LEN, HEADS, HEAD_DIM).astype(jnp.float32)
        scores = jnp.einsum('bqhd,bkhd->bhqk', query_heads, key_float, precision=highest) * score_scale
        raised = jnp.exp(scores)
        probabilities = raised / lax.optimization_barrier(jnp.sum(raised, axis=-1, keepdims=True))
        rounded_probs = lax.optimization_barrier(probabilities.astype(jnp.bfloat16)).astype(jnp.float32)
        group_out = jnp.einsum('bhqk,bkhd->bqhd', rounded_probs, value_float, precision=highest).astype(jnp.bfloat16)
        slope_grad = jnp.einsum('bqhd,bkhd->bhqk', grad_heads, value_float, precision=highest)
        row_delta = lax.optimization_barrier(jnp.sum(probabilities * slope_grad, axis=-1, keepdims=True))
        shaped_grad = lax.optimization_barrier((probabilities * (slope_grad - row_delta)).astype(jnp.bfloat16)).astype(jnp.float32)
        group_dq = (jnp.einsum('bhqk,bkhd->bqhd', shaped_grad, key_float, precision=highest) * score_scale).astype(jnp.bfloat16)
        key_piece = jnp.einsum('bhqk,bqhd->bkhd', shaped_grad, query_heads, precision=highest) * score_scale
        value_piece = jnp.einsum('bhqk,bqhd->bkhd', rounded_probs, grad_heads, precision=highest)
        key_total = totals[0].at[flat_pair].add(key_piece.reshape(group_size * 2, NBR_LEN, D))
        value_total = totals[1].at[flat_pair].add(value_piece.reshape(group_size * 2, NBR_LEN, D))
        return ((key_total, value_total), (group_out.reshape(group_size, BLOCK_LEN, D), group_dq.reshape(group_size, BLOCK_LEN, D)))
    start_totals = (jnp.zeros((ENTRIES, NBR_LEN, D), jnp.float32), jnp.zeros((ENTRIES, NBR_LEN, D), jnp.float32))
    totals, results = lax.scan(step, start_totals, (query_groups, grad_groups, pair_groups))
    attended = ungrouped(results[0], sequence_count, offset_rows)
    query_grad = ungrouped(results[1], sequence_count, offset_rows)
    key_grad = totals[0].astype(jnp.bfloat16).reshape(ENTRIES * NBR_LEN, D)
    value_grad = totals[1].astype(jnp.bfloat16).reshape(ENTRIES * NBR_LEN, D)
    summed = jnp.dot(key_grad, key_weight.T, preferred_element_type=jnp.float32)
    summed = summed + jnp.dot(value_grad, value_weight.T, preferred_element_type=jnp.float32)
    neighbour_grad = summed.astype(jnp.bfloat16).reshape(ENTRIES, NBR_LEN, ENC)
    return (attended, query_grad, neighbour_grad)
```

```python
import functools
import math

import jax
import jax.numpy as jnp
from jax import lax
from jax.experimental import pallas as pl
from jax.experimental.pallas import tpu as pltpu
from jax.sharding import PartitionSpec as P

HEAD_DIM = 128
BLOCK_LEN = 64
SEQ_LEN = 2048
Z_SIZE, Y_SIZE, X_SIZE, CORES = 8, 4, 4, 2
PARTS = ((0, 512), (512, 384))
GRAD_PARTS = ((0, 64), (64, 48))
GROUPS = 2
STEP_BLOCKS = 2
VMEM_LIMIT = 56 * 1024 * 1024


def receive_z(block, k):
    route = [
        (((z + k) % Z_SIZE) * Y_SIZE + y, z * Y_SIZE + y)
        for z in range(Z_SIZE)
        for y in range(Y_SIZE)
    ]
    return lax.ppermute(block, "seq", route)


def receive_y(block, k):
    route = [
        (z * Y_SIZE + (y + k) % Y_SIZE, z * Y_SIZE + y)
        for z in range(Z_SIZE)
        for y in range(Y_SIZE)
    ]
    return lax.ppermute(block, "seq", route)


def receive_x(block, k):
    route = [
        (((x + k) % X_SIZE) * CORES + c, x * CORES + c)
        for x in range(X_SIZE)
        for c in range(CORES)
    ]
    return lax.ppermute(block, "tensor", route)


def other_core(block):
    route = [
        (x * CORES + 1 - c, x * CORES + c) for x in range(X_SIZE) for c in range(CORES)
    ]
    return lax.ppermute(block, "tensor", route)


def ring_gather(own, receive, size):
    half = size // 2
    middle = own.shape[0] // 2
    got = {0: own}
    up = down = own
    for distance in range(1, half):
        up, down = receive(up, 1), receive(down, -1)
        got[distance], got[size - distance] = up, down
    first, second = receive(up[:middle], 1), receive(down[middle:], -1)
    return got, first, second


def add(*terms):
    total = terms[0].astype(jnp.float32)
    for term in terms[1:]:
        total = total + term.astype(jnp.float32)
    return total.astype(jnp.bfloat16)


def ring_scatter(near, first, second, receive, size):
    half = size // 2
    middle = first.shape[0]
    up, down = receive(first, -1), receive(second, 1)
    for distance in range(half - 1, 0, -1):
        ahead, behind = near[distance], near[size - distance]
        if distance == half - 1:
            ahead = jnp.concatenate([add(ahead[:middle], up), ahead[middle:]])
            behind = jnp.concatenate([behind[:middle], add(behind[middle:], down)])
        else:
            ahead, behind = add(ahead, up), add(behind, down)
        up, down = receive(ahead, -1), receive(behind, 1)
    return add(near[0], up, down)


def tables_of(z_first, plan):
    far_z, far_y, local, entries = plan
    if z_first:
        row, far, ring = far_z * entries + local, far_y, Y_SIZE
        middle = Z_SIZE * entries // 2
    else:
        row, far, ring = far_y * entries + local, far_z, Z_SIZE
        middle = Y_SIZE * entries // 2
    half = ring // 2
    late = row >= middle
    table = jnp.where(far < half, far, far - 1)
    table = jnp.where(far == half, jnp.where(late, ring, ring - 1), table)
    row = jnp.where((far == half) & late, row - middle, row)
    return table.astype(jnp.int32), row.astype(jnp.int32)


def pick_kernel(count, table_ref, row_ref, *refs):
    *sources, picked, sem = refs

    def one(i, carry):
        for k, source in enumerate(sources):

            @pl.when(table_ref[i] == k)
            def _():
                pltpu.make_async_copy(source.at[row_ref[i]], picked.at[i], sem).start()

        return carry

    lax.fori_loop(0, count, one, 0)
    pltpu.make_async_copy(picked, picked, sem).wait()


def pick(sources, table, row):
    count = table.shape[0]
    shape = (count,) + sources[0].shape[1:]
    return pl.pallas_call(
        functools.partial(pick_kernel, count),
        out_shape=jax.ShapeDtypeStruct(shape, jnp.bfloat16),
        in_specs=[pl.BlockSpec(memory_space=pltpu.SMEM)] * 2
        + [pl.BlockSpec(memory_space=pl.ANY)] * len(sources),
        out_specs=pl.BlockSpec(memory_space=pl.ANY),
        scratch_shapes=[pltpu.SemaphoreType.DMA],
        name="pick",
    )(table, row, *sources)


def place_kernel(count, table_ref, row_ref, given, *outs):
    for out in outs:

        def clear(i, carry, out=out):
            out[i] = jnp.zeros(out.shape[1:], out.dtype)
            return carry

        lax.fori_loop(0, out.shape[0], clear, 0)

    def one(i, carry):
        for k, out in enumerate(outs):

            @pl.when(table_ref[i] == k)
            def _():
                row = row_ref[i]
                total = out[row].astype(jnp.float32) + given[i].astype(jnp.float32)
                out[row] = total.astype(out.dtype)

        return carry

    lax.fori_loop(0, count, one, 0)


def place(given, sizes, table, row):
    count = given.shape[0]
    shapes = [jax.ShapeDtypeStruct((size,) + given.shape[1:], jnp.bfloat16) for size in sizes]
    return pl.pallas_call(
        functools.partial(place_kernel, count),
        out_shape=shapes,
        in_specs=[pl.BlockSpec(memory_space=pltpu.SMEM)] * 2
        + [pl.BlockSpec(memory_space=pltpu.VMEM)],
        out_specs=[pl.BlockSpec(memory_space=pltpu.VMEM)] * len(sizes),
        compiler_params=pltpu.CompilerParams(vmem_limit_bytes=VMEM_LIMIT),
        name="place",
    )(table, row, given)


def nt(a, b):
    return lax.dot_general(a, b, (((1,), (1,)), ((), ())), preferred_element_type=jnp.float32)


def tn(a, b):
    return lax.dot_general(a, b, (((0,), (0,)), ((), ())), preferred_element_type=jnp.float32)


def nn(a, b):
    return jnp.dot(a, b, preferred_element_type=jnp.float32)


def attention_kernel(place_ref, q_ref, g_ref, w_ref, *refs, heads, part_widths, grad_parts, share):
    n_peers = X_SIZE * CORES
    n_in = n_peers * len(part_widths)
    pieces, outs = refs[:n_in], refs[n_in:]
    out_ref, dq_ref = outs[0], outs[1]
    grad_refs = outs[2 : 2 + CORES * len(grad_parts)]
    rows_ref, grad_ref = outs[-2], outs[-1]
    entries = pieces[0].shape[0]
    part_rows = pieces[0].shape[1]
    nbr = n_peers * part_rows
    width = heads * HEAD_DIM
    scale = 1.0 / math.sqrt(HEAD_DIM)
    for peer in range(n_peers):
        start = pl.multiple_of(place_ref[peer] * part_rows, part_rows)
        lo = 0
        for part, part_width in enumerate(part_widths):
            piece = pieces[part * n_peers + peer]
            for e in range(entries):
                rows_ref[e, pl.ds(start, part_rows), lo : lo + part_width] = piece[e]
            lo += part_width
    for b in range(entries // 2):
        rows = rows_ref[2 * b : 2 * b + 2].reshape(2 * nbr, -1)
        both = nn(rows, w_ref[...]).astype(jnp.bfloat16)
        token = slice(b * BLOCK_LEN, (b + 1) * BLOCK_LEN)
        dk, dv = [], []
        for h in range(heads):
            cols = slice(h * HEAD_DIM, (h + 1) * HEAD_DIM)
            q, g = q_ref[token, cols], g_ref[token, cols]
            k, v = both[:, cols], both[:, width + h * HEAD_DIM : width + (h + 1) * HEAD_DIM]
            raised = jnp.exp(nt(q, k) * scale)
            probs = raised / jnp.sum(raised, axis=-1, keepdims=True)
            rounded = probs.astype(jnp.bfloat16)
            slope = nt(g, v)
            delta = jnp.sum(probs * slope, axis=-1, keepdims=True)
            shaped = (probs * (slope - delta)).astype(jnp.bfloat16)
            out_ref[token, cols] = nn(rounded, v).astype(jnp.bfloat16)
            dq_ref[token, cols] = (nn(shaped, k) * scale).astype(jnp.bfloat16)
            dk.append((tn(q, shaped) * scale).astype(jnp.bfloat16))
            dv.append(tn(g, rounded).astype(jnp.bfloat16))
        stacked = jnp.concatenate(dk + dv, axis=0)
        grad_ref[...] = nn(w_ref[...], stacked).astype(jnp.bfloat16)
        for peer in range(n_peers):
            across, core = peer // CORES, peer % CORES
            for part, (lo, part_width) in enumerate(grad_parts):
                start = pl.multiple_of(place_ref[peer] * share + lo, 16)
                piece = grad_ref[pl.ds(start, part_width), :]
                target = grad_refs[part * CORES + core]
                target[across, 2 * b] = piece[:, :nbr]
                target[across, 2 * b + 1] = piece[:, nbr:]


def attention(peers, queries, cotangent, weights, pieces, group, share):
    features = queries.shape[1]
    heads = features // HEAD_DIM
    entries, part_rows = pieces[0][0].shape[:2]
    nbr = len(pieces[0]) * part_rows
    blocks = entries // 2
    steps = blocks // STEP_BLOCKS
    token_rows = STEP_BLOCKS * BLOCK_LEN
    first = group * steps
    part_widths = tuple(part[0].shape[2] for part in pieces)
    flat = [piece for part in pieces for piece in part]
    token_in = pl.BlockSpec((token_rows, features), lambda i, s: (first + i, 0))
    token_out = pl.BlockSpec((token_rows, features), lambda i, s: (i, 0))
    out_shape = [jax.ShapeDtypeStruct((blocks * BLOCK_LEN, features), jnp.bfloat16)] * 2
    out_specs = [token_out] * 2
    for _, width in GRAD_PARTS:
        for _ in range(CORES):
            out_shape.append(jax.ShapeDtypeStruct((X_SIZE, entries, width, nbr), jnp.bfloat16))
            out_specs.append(
                pl.BlockSpec((X_SIZE, 2 * STEP_BLOCKS, width, nbr), lambda i, s: (0, i, 0, 0))
            )
    flops = blocks * (2 * 2 * 2 * nbr * sum(part_widths) * 2 * features + 12 * BLOCK_LEN * 2 * nbr * features)
    moved = 2 * 4 * entries * nbr * sum(part_widths)
    return pl.pallas_call(
        functools.partial(
            attention_kernel,
            heads=heads,
            part_widths=part_widths,
            grad_parts=GRAD_PARTS,
            share=share,
        ),
        out_shape=out_shape,
        grid_spec=pltpu.PrefetchScalarGridSpec(
            num_scalar_prefetch=1,
            grid=(steps,),
            in_specs=[
                token_in,
                token_in,
                pl.BlockSpec(weights.shape, lambda i, s: (0, 0)),
            ]
            + [
                pl.BlockSpec((2 * STEP_BLOCKS,) + piece.shape[1:], lambda i, s: (i, 0, 0))
                for piece in flat
            ],
            out_specs=out_specs,
            scratch_shapes=[
                pltpu.VMEM((2 * STEP_BLOCKS, nbr, sum(part_widths)), jnp.bfloat16),
                pltpu.VMEM((sum(part_widths), 2 * nbr), jnp.bfloat16),
            ],
        ),
        compiler_params=pltpu.CompilerParams(vmem_limit_bytes=VMEM_LIMIT),
        cost_estimate=pl.CostEstimate(flops=2 * flops, bytes_accessed=moved, transcendentals=0),
        name="attend",
    )(peers, queries, cotangent, weights, *flat)


def gather_x(own, group):
    ahead, behind = receive_x(own, 1), receive_x(own, -1)
    far = receive_x(ahead, 1) if group % 2 == 0 else receive_x(behind, -1)
    same = [own, ahead, far, behind]
    pieces = []
    for piece in same:
        pieces += [piece, other_core(piece)]
    return pieces


def scatter_x(kept, sent, group):
    came = other_core(sent)
    near = [add(kept[d], came[d]) for d in range(X_SIZE)]
    if group % 2 == 0:
        up = receive_x(add(near[1], receive_x(near[2], -1)), -1)
        down = receive_x(near[3], 1)
    else:
        up = receive_x(near[1], -1)
        down = receive_x(add(near[3], receive_x(near[2], 1)), 1)
    return add(near[0], up, down)


def gather_seq(own, z_first):
    first_ring, second_ring = ((receive_z, Z_SIZE), (receive_y, Y_SIZE)) if z_first else ((receive_y, Y_SIZE), (receive_z, Z_SIZE))
    got, first, second = ring_gather(own, *first_ring)
    size = first_ring[1]
    order = [got[d] for d in range(size // 2)] + [first, second] + [got[d] for d in range(size // 2 + 1, size)]
    line = jnp.concatenate(order, axis=0)
    got, first, second = ring_gather(line, *second_ring)
    return [got[d] for d in sorted(got)] + [first, second]


def scatter_seq(tables, z_first):
    first_ring, second_ring = ((receive_y, Y_SIZE), (receive_z, Z_SIZE)) if z_first else ((receive_z, Z_SIZE), (receive_y, Y_SIZE))
    size = first_ring[1]
    distances = [d for d in range(size) if d != size // 2]
    near = dict(zip(distances, tables[:-2]))
    line = ring_scatter(near, tables[-2], tables[-1], *first_ring)
    size = second_ring[1]
    entries = line.shape[0] // size
    near = {d: line[d * entries : (d + 1) * entries] for d in range(size) if d != size // 2}
    start, middle = size // 2 * entries, entries // 2
    return ring_scatter(
        near, line[start : start + middle], line[start + middle : start + entries], *second_ring
    )


def table_sizes(z_first, entries):
    line, ring = (Z_SIZE, Y_SIZE) if z_first else (Y_SIZE, Z_SIZE)
    return [line * entries] * (ring - 1) + [line * entries // 2] * 2


def shards(queries, cotangent, neighbours, key_weight, value_weight, retrieval):
    token_rows, features = queries.shape
    entries, nbr, encoder = neighbours.shape
    peers_count = X_SIZE * CORES
    seq_index, tensor_index = lax.axis_index("seq"), lax.axis_index("tensor")
    offset_rows = BLOCK_LEN - 1
    sequence_devices = SEQ_LEN // token_rows
    seq_size = Z_SIZE * Y_SIZE
    inside = [(i, i + 1) for i in range(seq_size) if (i + 1) % sequence_devices]

    leading = jnp.stack([queries[:offset_rows], cotangent[:offset_rows]])
    arrived = lax.ppermute(leading, "seq", [(b, a) for a, b in inside])
    query_ext = jnp.concatenate([queries[offset_rows:], arrived[0]], axis=0)
    grad_ext = jnp.concatenate([cotangent[offset_rows:], arrived[1]], axis=0)
    weights = jnp.concatenate([key_weight, value_weight], axis=1)

    used = retrieval.reshape(-1)
    holder, local = used // entries, used % entries
    far_z = (holder // Y_SIZE - seq_index // Y_SIZE) % Z_SIZE
    far_y = (holder % Y_SIZE - seq_index % Y_SIZE) % Y_SIZE
    plan = (far_z, far_y, local, entries)
    spots = [tables_of(True, plan), tables_of(False, plan)]

    x_index, core = tensor_index // CORES, tensor_index % CORES
    peers = jnp.stack(
        [((x_index + dx) % X_SIZE) * CORES + (core + dc) % CORES for dx in range(X_SIZE) for dc in range(CORES)]
    ).astype(jnp.int32)

    part_rows = nbr // peers_count
    mine = lax.dynamic_slice_in_dim(neighbours, tensor_index * part_rows, part_rows, axis=1)
    group_entries = used.shape[0] // GROUPS
    picked = []
    for part, (lo, width) in enumerate(PARTS):
        tables = gather_seq(mine[:, :, lo : lo + width], part == 0)
        picked.append(pick(tables, *spots[part]))

    results, summed = [], [[] for _ in GRAD_PARTS]
    for group in range(GROUPS):
        span = slice(group * group_entries, (group + 1) * group_entries)
        pieces = [gather_x(part[span], group) for part in picked]
        out, dq, *grads = attention(
            peers, query_ext, grad_ext, weights, pieces, group, encoder // peers_count
        )
        results.append((out, dq))
        for part in range(len(GRAD_PARTS)):
            kept, sent = grads[part * CORES : (part + 1) * CORES]
            summed[part].append(scatter_x(kept, sent, group))

    settled = []
    for which in range(2):
        extended = jnp.concatenate([pair[which] for pair in results], axis=0)
        carried = lax.ppermute(extended[token_rows - offset_rows :], "seq", inside)
        settled.append(jnp.concatenate([carried, extended[: token_rows - offset_rows]], axis=0))

    shares = []
    for part in range(len(GRAD_PARTS)):
        z_first = part == 0
        tables = place(
            jnp.concatenate(summed[part], axis=0), table_sizes(z_first, entries), *spots[part]
        )
        shares.append(scatter_seq(tables, z_first))
    neighbour_grad = jnp.concatenate(shares, axis=1).transpose(0, 2, 1)
    return settled[0], settled[1], neighbour_grad


def solution(mesh):
    placed = (
        P("seq", "tensor"),
        P("seq", "tensor"),
        P("seq", None, None),
        P(None, "tensor"),
        P(None, "tensor"),
        P("seq", None),
    )
    return jax.shard_map(
        shards,
        mesh=mesh,
        in_specs=placed,
        out_specs=(P("seq", "tensor"), P("seq", "tensor"), P("seq", None, "tensor")),
        check_vma=False,
    )
```

```python
import functools
import math

import jax
import jax.numpy as jnp
from jax import lax
from jax.experimental import pallas as pl
from jax.experimental.pallas import tpu as pltpu
from jax.sharding import Mesh
from jax.sharding import PartitionSpec as P

HEAD_DIM = 128
BLOCK_LEN = 64
SEQ_LEN = 2048
Z_SIZE, Y_SIZE, X_SIZE, CORES = 8, 4, 4, 2
PARTS = ((0, 512), (512, 384))
GRAD_PARTS = ((0, 64), (64, 48))
NEAR_Z, FAR_Z = (0, 1, 2, 6, 7), (3, 4, 5)
GROUPS = 2
ENTRIES_DEV = 8
STEP_BLOCKS = 2
TOKEN_STEPS = 4
VMEM_LIMIT = 56 * 1024 * 1024


def receive_on(axis, size):
    def receive(block, k):
        return lax.ppermute(block, axis, [((i + k) % size, i) for i in range(size)])

    return receive


receive_z = receive_on("z", Z_SIZE)
receive_y = receive_on("y", Y_SIZE)
receive_x = receive_on("x", X_SIZE)
other_core = functools.partial(receive_on("core", CORES), k=1)


def after(blocks, earlier):
    return lax.optimization_barrier((blocks, earlier))[0]


def straight_gather(own, receive, size):
    return [own] + [receive(own, k) for k in range(1, size)]


def straight_scatter(terms, receive, size):
    return add(terms[0], *[receive(terms[k], -k) for k in range(1, size)])


def add(*terms):
    total = terms[0].astype(jnp.float32)
    for term in terms[1:]:
        total = total + term.astype(jnp.float32)
    return total.astype(jnp.bfloat16)


def used_entry(pairs_ref, i, count):
    core = lax.axis_index("core")
    half = count // CORES
    turned = lax.rem(core * half + i, count)
    entry = pairs_ref[turned // 2, lax.rem(turned, 2)]
    holder, local = entry // ENTRIES_DEV, lax.rem(entry, ENTRIES_DEV)
    z, y = holder // Y_SIZE, lax.rem(holder, Y_SIZE)
    far_z = lax.rem(z + Z_SIZE - lax.axis_index("z"), Z_SIZE)
    far_y = lax.rem(y + Y_SIZE - lax.axis_index("y"), Y_SIZE)
    return z, far_z, far_y, local


def line_spot(far_z, far_y, local):
    line = jnp.int32(0)
    place = jnp.int32(0)
    for which, distances in enumerate((NEAR_Z, FAR_Z)):
        for i, d in enumerate(distances):
            line = jnp.where(far_z == d, which, line)
            place = jnp.where(far_z == d, i, place)
    row, half = place * ENTRIES_DEV + local, Y_SIZE // 2
    middle = jnp.where(line == 1, len(FAR_Z), len(NEAR_Z)) * ENTRIES_DEV // 2
    late = jnp.logical_and(far_y == half, row >= middle)
    table = jnp.where(far_y < half, far_y, far_y - 1)
    table = jnp.where(far_y == half, jnp.where(late, Y_SIZE, Y_SIZE - 1), table)
    return line, table, jnp.where(late, row - middle, row)


def at_spots(pairs_ref, i, count, tables, act):
    z, far_z, far_y, local = used_entry(pairs_ref, i, count)
    line, table, row = line_spot(far_z, far_y, local)
    for which in range(2):

        @pl.when(line == which)
        def _():
            for k in range(Y_SIZE + 1):

                @pl.when(table == k)
                def _(held=tables[which * (Y_SIZE + 1) + k]):
                    act(0, held, row)

    act(1, tables[-1], (z * Y_SIZE + far_y) * ENTRIES_DEV + local)


def pick_kernel(count, pairs_ref, *refs):
    tables, outs = refs[:-CORES], refs[-CORES:]
    starts = [lo for lo, _ in PARTS]

    def one(i, carry, picked, first):
        def act(part, held, row):
            lo = starts[part]
            picked[i, :, lo : lo + held.shape[2]] = held[row]

        at_spots(pairs_ref, first + i, count, tables, act)
        return carry

    half = count // CORES
    for core in range(CORES):
        lax.fori_loop(0, half, functools.partial(one, picked=outs[core], first=core * half), 0)


def pick(tables, pairs):
    count = pairs.size
    width = sum(width for _, width in PARTS)
    shape = jax.ShapeDtypeStruct((count // CORES, tables[0].shape[1], width), jnp.bfloat16)
    return pl.pallas_call(
        functools.partial(pick_kernel, count),
        out_shape=[shape] * CORES,
        in_specs=[pl.BlockSpec(memory_space=pltpu.SMEM)] + [pl.BlockSpec(memory_space=pltpu.VMEM)] * len(tables),
        out_specs=[pl.BlockSpec(memory_space=pltpu.VMEM)] * CORES,
        compiler_params=pltpu.CompilerParams(vmem_limit_bytes=VMEM_LIMIT),
        name="pick",
    )(pairs, *tables)


CLEAR_ROWS = 4


def place_kernel(count, pairs_ref, *refs):
    given, tables = refs[:CORES], refs[CORES:]
    for table in tables:

        def clear(i, carry, table=table):
            table[pl.ds(i * CLEAR_ROWS, CLEAR_ROWS)] = jnp.zeros((CLEAR_ROWS,) + table.shape[1:], table.dtype)
            return carry

        lax.fori_loop(0, table.shape[0] // CLEAR_ROWS, clear, 0)
    starts = [lo for lo, _ in GRAD_PARTS]

    def one(i, carry, terms, first):
        def act(part, held, row):
            lo = starts[part]
            term = terms[i, lo : lo + held.shape[1]].astype(jnp.float32)
            held[row] = (held[row].astype(jnp.float32) + term).astype(held.dtype)

        at_spots(pairs_ref, first + i, count, tables, act)
        return carry

    half = count // CORES
    for core in range(CORES):
        lax.fori_loop(0, half, functools.partial(one, terms=given[core], first=core * half), 0)


def place(given, pairs):
    nbr = given[0].shape[2]
    shapes = [
        jax.ShapeDtypeStruct((size, width, nbr), jnp.bfloat16)
        for (_, width), sizes in zip(GRAD_PARTS, table_sizes(ENTRIES_DEV))
        for size in sizes
    ]
    return pl.pallas_call(
        functools.partial(place_kernel, pairs.size),
        out_shape=shapes,
        in_specs=[pl.BlockSpec(memory_space=pltpu.SMEM)] + [pl.BlockSpec(memory_space=pltpu.VMEM)] * len(given),
        out_specs=[pl.BlockSpec(memory_space=pltpu.VMEM)] * len(shapes),
        compiler_params=pltpu.CompilerParams(vmem_limit_bytes=VMEM_LIMIT),
        name="place",
    )(pairs, *given)


def nt(a, b):
    return lax.dot_general(a, b, (((1,), (1,)), ((), ())), preferred_element_type=jnp.float32)


def tn(a, b):
    return lax.dot_general(a, b, (((0,), (0,)), ((), ())), preferred_element_type=jnp.float32)


def nn(a, b):
    return jnp.dot(a, b, preferred_element_type=jnp.float32)


def shifted(rows, following):
    rows = jnp.concatenate([rows.astype(jnp.float32), following.astype(jnp.float32)], axis=0)
    count = rows.shape[0]
    return pltpu.roll(rows, count - (BLOCK_LEN - 1), 0)[: count - BLOCK_LEN].astype(jnp.bfloat16)


def attention_kernel(place_ref, *refs, heads, share, first):
    token_refs, w_refs, refs = refs[:9], refs[9 : 9 + 2 * CORES], refs[9 + 2 * CORES :]
    pieces, outs = refs[:X_SIZE], refs[X_SIZE:]
    own_ref, other_ref = outs[:2]
    grad_refs = outs[2 : 2 + X_SIZE]
    rows_ref, grad_ref, w_ref = outs[-3:]
    *token_refs, arrived_ref = token_refs
    step = pl.program_id(0)
    last = place_ref[X_SIZE * CORES] * (TOKEN_STEPS) + first + step == CORES * TOKEN_STEPS - 1
    q_blocks, g_blocks = [], []
    for which, blocks in enumerate((q_blocks, g_blocks)):
        rows, following, their_rows, their_following = token_refs[4 * which : 4 * which + 4]
        blocks.append(shifted(rows[...], jnp.where(last, arrived_ref[which], following[...])))
        blocks.append(shifted(their_rows[0], their_following[0]))
    entries, part_rows = pieces[0].shape[1:3]
    nbr = X_SIZE * CORES * part_rows
    width = heads * HEAD_DIM
    scale = 1.0 / math.sqrt(HEAD_DIM)

    @pl.when(step == 0)
    def _():
        for i, ref in enumerate(w_refs):
            w_ref[:, i * width : (i + 1) * width] = ref[...]

    where = [(across, core) for across in range(X_SIZE) for core in range(CORES)]
    for across, core in where:
        start = pl.multiple_of(place_ref[across * CORES + core] * part_rows, part_rows)
        for e in range(entries):
            rows_ref[e, pl.ds(start, part_rows), :] = pieces[across][core, e]
    blocks = entries // 2
    rows = rows_ref[...].reshape(entries * nbr, -1)
    both = nn(rows, w_ref[...]).astype(jnp.bfloat16)
    jobs = [(b, c, h) for b in range(blocks) for c in range(CORES) for h in range(heads)]
    count = range(len(jobs))
    token = [slice(b * BLOCK_LEN, (b + 1) * BLOCK_LEN) for b, _, _ in jobs]
    cols = [slice(h * HEAD_DIM, (h + 1) * HEAD_DIM) for _, _, h in jobs]
    keys = [slice(b * 2 * nbr, (b + 1) * 2 * nbr) for b, _, _ in jobs]
    base = [2 * c * width + h * HEAD_DIM for _, c, h in jobs]
    q = [q_blocks[jobs[i][1]][token[i], cols[i]] for i in count]
    g = [g_blocks[jobs[i][1]][token[i], cols[i]] for i in count]
    k = [both[keys[i], base[i] : base[i] + HEAD_DIM] for i in count]
    v = [both[keys[i], width + base[i] : width + base[i] + HEAD_DIM] for i in count]
    scores = [nt(q[i], k[i]) for i in count]
    slope = [nt(g[i], v[i]) for i in count]
    raised = [jnp.exp(scores[i] * scale) for i in count]
    inverse = [1.0 / jnp.sum(raised[i], axis=-1, keepdims=True) for i in count]
    probs = [raised[i] * inverse[i] for i in count]
    rounded = [probs[i].astype(jnp.bfloat16) for i in count]
    delta = [jnp.sum(probs[i] * slope[i], axis=-1, keepdims=True) for i in count]
    shaped = [(probs[i] * (slope[i] - delta[i])).astype(jnp.bfloat16) for i in count]
    for i in count:
        result = (own_ref, other_ref)[jobs[i][1]]
        result[0, token[i], cols[i]] = nn(rounded[i], v[i]).astype(jnp.bfloat16)
        result[1, token[i], cols[i]] = (nn(shaped[i], k[i]) * scale).astype(jnp.bfloat16)
    dk = [(tn(q[i], shaped[i]) * scale).astype(jnp.bfloat16) for i in count]
    dv = [tn(g[i], rounded[i]).astype(jnp.bfloat16) for i in count]
    columns = []
    for b in range(blocks):
        terms = []
        for c in range(CORES):
            at = (b * CORES + c) * heads
            terms += dk[at : at + heads] + dv[at : at + heads]
        columns.append(jnp.concatenate(terms, axis=0))
    grad_ref[...] = nn(w_ref[...], jnp.concatenate(columns, axis=1)).astype(jnp.bfloat16)
    for across, core in where:
        start = pl.multiple_of(place_ref[across * CORES + core] * share, 16)
        terms = grad_ref[pl.ds(start, share), :]
        for e in range(entries):
            grad_refs[across][core, e] = terms[:, e * nbr : (e + 1) * nbr]


def attention(peers, tokens, others, arrived, weights, pieces, group, share):
    features = tokens[0].shape[1]
    heads = features // HEAD_DIM
    _, entries, part_rows, encoder = pieces[0].shape
    nbr = X_SIZE * CORES * part_rows
    blocks = entries // 2
    steps = blocks // STEP_BLOCKS
    token_rows = STEP_BLOCKS * BLOCK_LEN
    first = group * steps
    step_entries = 2 * STEP_BLOCKS
    end = tokens[0].shape[0] // BLOCK_LEN - 1

    def own_rows(i, s):
        return s[X_SIZE * CORES] * TOKEN_STEPS + first + i, 0

    def own_following(i, s):
        return jnp.minimum((s[X_SIZE * CORES] * TOKEN_STEPS + first + i + 1) * STEP_BLOCKS, end), 0

    in_specs = []
    for which in range(2):
        in_specs += [
            pl.BlockSpec((token_rows, features), own_rows),
            pl.BlockSpec((BLOCK_LEN, features), own_following),
            pl.BlockSpec((1, token_rows, features), lambda i, s, which=which: (which, first + i, 0)),
            pl.BlockSpec((1, BLOCK_LEN, features), lambda i, s, which=which: (which, (first + i + 1) * STEP_BLOCKS, 0)),
        ]
    in_specs.append(pl.BlockSpec(arrived.shape, lambda i, s: (0, 0, 0)))
    in_specs += [pl.BlockSpec(weight.shape, lambda i, s: (0, 0)) for weight in weights]
    in_specs += [
        pl.BlockSpec((CORES, step_entries) + piece.shape[2:], lambda i, s: (0, i, 0, 0)) for piece in pieces
    ]
    out_shape = [jax.ShapeDtypeStruct((2, blocks * BLOCK_LEN, features), jnp.bfloat16)] * CORES
    out_specs = [pl.BlockSpec((2, token_rows, features), lambda i, s: (0, i, 0))] * CORES
    for piece in pieces:
        out_shape.append(jax.ShapeDtypeStruct((piece.shape[0], entries, share, nbr), jnp.bfloat16))
        out_specs.append(pl.BlockSpec((piece.shape[0], step_entries, share, nbr), lambda i, s: (0, i, 0, 0)))
    flops = blocks * 2 * (2 * 2 * nbr * encoder * 2 * CORES * features + 6 * BLOCK_LEN * 2 * nbr * CORES * features)
    moved = 2 * 2 * entries * nbr * encoder + 4 * CORES * weights[0].size
    return pl.pallas_call(
        functools.partial(attention_kernel, heads=heads, share=share, first=first),
        out_shape=out_shape,
        grid_spec=pltpu.PrefetchScalarGridSpec(
            num_scalar_prefetch=1,
            grid=(steps,),
            in_specs=in_specs,
            out_specs=out_specs,
            scratch_shapes=[
                pltpu.VMEM((step_entries, nbr, encoder), jnp.bfloat16),
                pltpu.VMEM((encoder, step_entries * nbr), jnp.bfloat16),
                pltpu.VMEM((encoder, 2 * CORES * features), jnp.bfloat16),
            ],
        ),
        compiler_params=pltpu.CompilerParams(vmem_limit_bytes=VMEM_LIMIT),
        cost_estimate=pl.CostEstimate(flops=2 * flops, bytes_accessed=moved, transcendentals=0),
        name="attend",
    )(
        peers,
        *[array for own in tokens for array in (own, own, others, others)],
        arrived,
        *weights,
        *pieces,
    )


def gather_near(own):
    return {d: receive_z(own, d) if d else own for d in NEAR_Z}


def gather_lines(got):
    got = dict(got)
    near = jnp.concatenate([got[d] for d in NEAR_Z], axis=0)
    got[3], got[4], got[5] = receive_z(got[2], 1), receive_z(got[0], 4), receive_z(got[6], -1)
    near_up, near_down = receive_y(near, 1), receive_y(near, -1)
    near_up, near_down, *got = lax.optimization_barrier((near_up, near_down, got[3], got[4], got[5]))
    far = jnp.concatenate(got, axis=0)
    middle = near.shape[0] // 2
    near_halves = [receive_y(near_up[:middle], 1), receive_y(near_down[middle:], -1)]
    far_up, far_down = receive_y(far, 1), receive_y(far, -1)
    near_halves, far_up, far_down = lax.optimization_barrier((near_halves, far_up, far_down))
    middle = far.shape[0] // 2
    far_halves = [receive_y(far_up[:middle], 1), receive_y(far_down[middle:], -1)]
    return [near, near_up, near_down] + near_halves + [far, far_up, far_down] + far_halves


def ring_scatter(near, first, second, receive, size):
    half = size // 2
    middle = first.shape[0]
    up, down = receive(first, -1), receive(second, 1)
    for distance in range(half - 1, 0, -1):
        ahead, behind = near[distance], near[size - distance]
        if distance == half - 1:
            ahead = jnp.concatenate([add(ahead[:middle], up), ahead[middle:]])
            behind = jnp.concatenate([behind[:middle], add(behind[middle:], down)])
        else:
            ahead, behind = add(ahead, up), add(behind, down)
        up, down = receive(ahead, -1), receive(behind, 1)
    return add(near[0], up, down)


def scatter_lines(tables):
    near, far = [], []
    for line, part in ((far, tables[Y_SIZE + 1 :]), (near, tables[: Y_SIZE + 1])):
        distances = [d for d in range(Y_SIZE) if d != Y_SIZE // 2]
        line.append(ring_scatter(dict(zip(distances, part[:-2])), *part[-2:], receive_y, Y_SIZE))
    term = {}
    for line, distances in ((near[0], NEAR_Z), (far[0], FAR_Z)):
        entries = line.shape[0] // len(distances)
        for i, d in enumerate(distances):
            term[d] = line[i * entries : (i + 1) * entries]
    middle = entries // 2
    ahead, behind = receive_z(term[3], -1), receive_z(term[5], 1)
    first, second = receive_z(term[4][:middle], -2), receive_z(term[4][middle:], 2)
    ahead = add(term[2], ahead, jnp.concatenate([first, jnp.zeros_like(first)], axis=0))
    behind = add(term[6], behind, jnp.concatenate([jnp.zeros_like(second), second], axis=0))
    return add(
        term[0], receive_z(term[1], -1), receive_z(term[7], 1), receive_z(ahead, -2), receive_z(behind, 2)
    )


def gather_whole(own, earlier):
    line = jnp.concatenate(straight_gather(own, receive_y, Y_SIZE), axis=0)
    line = after(line, earlier)
    return [lax.all_gather(line, "z", axis=0, tiled=True)]


def scatter_whole(tables):
    line = lax.psum_scatter(tables[0], "z", scatter_dimension=0, tiled=True)
    entries = line.shape[0] // Y_SIZE
    terms = [line[d * entries : (d + 1) * entries] for d in range(Y_SIZE)]
    return straight_scatter(terms, receive_y, Y_SIZE)


def table_sizes(entries):
    lines = []
    for line in (NEAR_Z, FAR_Z):
        rows = len(line) * entries
        lines += [rows] * (Y_SIZE - 1) + [rows // 2] * 2
    return lines, [Z_SIZE * Y_SIZE * entries]


def shards(queries, cotangent, neighbours, key_weight, value_weight, retrieval):
    token_rows, features = queries.shape
    entries, nbr, encoder = neighbours.shape
    peers_count = X_SIZE * CORES
    z, y, x, core = (lax.axis_index(axis) for axis in ("z", "y", "x", "core"))
    tensor_index = x * CORES + core
    offset_rows = BLOCK_LEN - 1
    sequence_devices = SEQ_LEN // token_rows
    seq_axes, seq_size = ("z", "y"), Z_SIZE * Y_SIZE
    inside = [(i, i + 1) for i in range(seq_size) if (i + 1) % sequence_devices]

    part_rows, share = nbr // peers_count, encoder // peers_count
    mine = lax.dynamic_slice_in_dim(neighbours, tensor_index * part_rows, part_rows, axis=1)
    cut = [mine[:, :, lo : lo + width] for lo, width in PARTS]
    away_weights = [other_core(key_weight), other_core(value_weight)]
    weights = [key_weight, value_weight] + away_weights
    cut[0] = after(cut[0], away_weights)
    near = gather_near(cut[0])
    parts = [gather_lines(near), gather_whole(cut[1], [near[d] for d in NEAR_Z if d])]

    leading = jnp.stack([queries[:BLOCK_LEN], cotangent[:BLOCK_LEN]])
    arrived = lax.ppermute(leading, seq_axes, [(b, a) for a, b in inside])

    core_rows = token_rows // CORES
    away = (1 - core) * core_rows
    inner = jnp.stack([array[core_rows : core_rows + BLOCK_LEN] for array in (queries, cotangent)])
    others = other_core(
        jnp.concatenate(
            [
                jnp.stack([lax.dynamic_slice_in_dim(array, away, core_rows) for array in (queries, cotangent)]),
                jnp.where(core == 1, inner, arrived),
            ],
            axis=1,
        )
    )
    peers = jnp.stack(
        [((x + dx) % X_SIZE) * CORES + (core + dc) % CORES for dx in range(X_SIZE) for dc in range(CORES)] + [core]
    ).astype(jnp.int32)

    kept, sent = pick(parts[0] + parts[1], retrieval)
    came = other_core(sent)
    group_entries = kept.shape[0] // GROUPS

    results, summed, pieces = [], [], None
    both = jnp.stack([kept, came])
    for group in range(GROUPS):
        held = both[:, group * group_entries : (group + 1) * group_entries]
        if pieces is not None:
            held = after(held, pieces[1:])
        pieces = straight_gather(held, receive_x, X_SIZE)
        own, other, *grads = attention(
            peers, (queries, cotangent), others, arrived, weights, pieces, group, share
        )
        results.append((own, other))
        summed.append(straight_scatter(grads, receive_x, X_SIZE))

    own, other = (jnp.concatenate(pair, axis=1) for pair in zip(*results))
    back = other_core(other)
    extended = jnp.where(core == 0, jnp.concatenate([own, back], axis=1), jnp.concatenate([back, own], axis=1))
    carried = lax.ppermute(extended[:, token_rows - offset_rows :], seq_axes, inside)
    settled = [
        jnp.concatenate([carried[which], extended[which, : token_rows - offset_rows]], axis=0) for which in range(2)
    ]

    summed = jnp.concatenate(summed, axis=1)
    tables = place([summed[0], other_core(summed[1])], retrieval)
    shares = [scatter_lines(tables[:-1]), scatter_whole(tables[-1:])]
    neighbour_grad = jnp.concatenate(shares, axis=1).transpose(0, 2, 1)
    return settled[0], settled[1], neighbour_grad


def solution(mesh):
    axes = Mesh(mesh.devices.reshape(Z_SIZE, Y_SIZE, X_SIZE, CORES), ("z", "y", "x", "core"))
    seq, tensor = ("z", "y"), ("x", "core")
    placed = (
        P(seq, tensor),
        P(seq, tensor),
        P(seq, None, None),
        P(None, tensor),
        P(None, tensor),
        P(seq, None),
    )
    return jax.shard_map(
        shards,
        mesh=axes,
        in_specs=placed,
        out_specs=(P(seq, tensor), P(seq, tensor), P(seq, None, tensor)),
        check_vma=False,
    )
```

```python
import functools
import math

import jax
import jax.numpy as jnp
from jax import lax
from jax.experimental import pallas as pl
from jax.experimental.pallas import tpu as pltpu
from jax.sharding import Mesh
from jax.sharding import PartitionSpec as P

HEAD_DIM = 128
BLOCK_LEN = 64
SEQ_LEN = 2048
Z_SIZE, Y_SIZE, X_SIZE, CORES = 8, 4, 4, 2
PARTS = ((0, 512), (512, 384))
GRAD_PARTS = ((0, 64), (64, 48))
NEAR_Z, FAR_Z = (0, 1, 2, 6, 7), (3, 4, 5)
GROUPS = 2
ENTRIES_DEV = 8
STEP_BLOCKS = 4
TOKEN_STEPS = 2
VMEM_LIMIT = 56 * 1024 * 1024


def receive_on(axis, size):
    def receive(block, k):
        return lax.ppermute(block, axis, [((i + k) % size, i) for i in range(size)])

    return receive


receive_z = receive_on("z", Z_SIZE)
receive_y = receive_on("y", Y_SIZE)
receive_x = receive_on("x", X_SIZE)
other_core = functools.partial(receive_on("core", CORES), k=1)


def after(blocks, earlier):
    return lax.optimization_barrier((blocks, earlier))[0]


def straight_gather(own, receive, size):
    return [own] + [receive(own, k) for k in range(1, size)]


def straight_scatter(terms, receive, size):
    return add(terms[0], *[receive(terms[k], -k) for k in range(1, size)])


def add(*terms):
    total = terms[0].astype(jnp.float32)
    for term in terms[1:]:
        total = total + term.astype(jnp.float32)
    return total.astype(jnp.bfloat16)


def used_entry(pairs_ref, i, count):
    core = lax.axis_index("core")
    half = count // CORES
    turned = lax.rem(core * half + i, count)
    entry = pairs_ref[turned // 2, lax.rem(turned, 2)]
    holder, local = entry // ENTRIES_DEV, lax.rem(entry, ENTRIES_DEV)
    z, y = holder // Y_SIZE, lax.rem(holder, Y_SIZE)
    far_z = lax.rem(z + Z_SIZE - lax.axis_index("z"), Z_SIZE)
    far_y = lax.rem(y + Y_SIZE - lax.axis_index("y"), Y_SIZE)
    return z, far_z, far_y, local


def line_spot(far_z, far_y, local):
    line = jnp.int32(0)
    place = jnp.int32(0)
    for which, distances in enumerate((NEAR_Z, FAR_Z)):
        for i, d in enumerate(distances):
            line = jnp.where(far_z == d, which, line)
            place = jnp.where(far_z == d, i, place)
    row, half = place * ENTRIES_DEV + local, Y_SIZE // 2
    middle = jnp.where(line == 1, len(FAR_Z), len(NEAR_Z)) * ENTRIES_DEV // 2
    late = jnp.logical_and(far_y == half, row >= middle)
    table = jnp.where(far_y < half, far_y, far_y - 1)
    table = jnp.where(far_y == half, jnp.where(late, Y_SIZE, Y_SIZE - 1), table)
    return line, table, jnp.where(late, row - middle, row)


def at_spots(pairs_ref, i, count, tables, act):
    z, far_z, far_y, local = used_entry(pairs_ref, i, count)
    line, table, row = line_spot(far_z, far_y, local)
    for which in range(2):

        @pl.when(line == which)
        def _():
            for k in range(Y_SIZE + 1):

                @pl.when(table == k)
                def _(held=tables[which * (Y_SIZE + 1) + k]):
                    act(0, held, row)

    act(1, tables[-1], (z * Y_SIZE + far_y) * ENTRIES_DEV + local)


def pick_kernel(count, pairs_ref, *refs):
    tables, outs = refs[:-CORES], refs[-CORES:]
    starts = [lo for lo, _ in PARTS]

    def one(i, carry, picked, first):
        def act(part, held, row):
            lo = starts[part]
            picked[i, :, lo : lo + held.shape[2]] = held[row]

        at_spots(pairs_ref, first + i, count, tables, act)
        return carry

    half = count // CORES
    for core in range(CORES):
        lax.fori_loop(0, half, functools.partial(one, picked=outs[core], first=core * half), 0)


def pick(tables, pairs):
    count = pairs.size
    width = sum(width for _, width in PARTS)
    shape = jax.ShapeDtypeStruct((count // CORES, tables[0].shape[1], width), jnp.bfloat16)
    return pl.pallas_call(
        functools.partial(pick_kernel, count),
        out_shape=[shape] * CORES,
        in_specs=[pl.BlockSpec(memory_space=pltpu.SMEM)] + [pl.BlockSpec(memory_space=pltpu.VMEM)] * len(tables),
        out_specs=[pl.BlockSpec(memory_space=pltpu.VMEM)] * CORES,
        compiler_params=pltpu.CompilerParams(vmem_limit_bytes=VMEM_LIMIT),
        name="pick",
    )(pairs, *tables)


CLEAR_ROWS = 4


def place_kernel(count, pairs_ref, *refs):
    given, tables = refs[:CORES], refs[CORES:]
    for table in tables:

        def clear(i, carry, table=table):
            table[pl.ds(i * CLEAR_ROWS, CLEAR_ROWS)] = jnp.zeros((CLEAR_ROWS,) + table.shape[1:], table.dtype)
            return carry

        lax.fori_loop(0, table.shape[0] // CLEAR_ROWS, clear, 0)
    starts = [lo for lo, _ in GRAD_PARTS]

    def one(i, carry, terms, first):
        def act(part, held, row):
            lo = starts[part]
            term = terms[i, lo : lo + held.shape[1]].astype(jnp.float32)
            held[row] = (held[row].astype(jnp.float32) + term).astype(held.dtype)

        at_spots(pairs_ref, first + i, count, tables, act)
        return carry

    half = count // CORES
    for core in range(CORES):
        lax.fori_loop(0, half, functools.partial(one, terms=given[core], first=core * half), 0)


def place(given, pairs):
    nbr = given[0].shape[2]
    shapes = [
        jax.ShapeDtypeStruct((size, width, nbr), jnp.bfloat16)
        for (_, width), sizes in zip(GRAD_PARTS, table_sizes(ENTRIES_DEV))
        for size in sizes
    ]
    return pl.pallas_call(
        functools.partial(place_kernel, pairs.size),
        out_shape=shapes,
        in_specs=[pl.BlockSpec(memory_space=pltpu.SMEM)] + [pl.BlockSpec(memory_space=pltpu.VMEM)] * len(given),
        out_specs=[pl.BlockSpec(memory_space=pltpu.VMEM)] * len(shapes),
        compiler_params=pltpu.CompilerParams(vmem_limit_bytes=VMEM_LIMIT),
        name="place",
    )(pairs, *given)


def nt(a, b):
    return lax.dot_general(a, b, (((1,), (1,)), ((), ())), preferred_element_type=jnp.float32)


def tn(a, b):
    return lax.dot_general(a, b, (((0,), (0,)), ((), ())), preferred_element_type=jnp.float32)


def nn(a, b):
    return jnp.dot(a, b, preferred_element_type=jnp.float32)


def shifted(rows, following):
    rows = jnp.concatenate([rows.astype(jnp.float32), following.astype(jnp.float32)], axis=0)
    count = rows.shape[0]
    return pltpu.roll(rows, count - (BLOCK_LEN - 1), 0)[: count - BLOCK_LEN].astype(jnp.bfloat16)


def attention_kernel(place_ref, *refs, heads, share, first):
    token_refs, w_refs, refs = refs[:9], refs[9 : 9 + 2 * CORES], refs[9 + 2 * CORES :]
    pieces, outs = refs[:X_SIZE], refs[X_SIZE:]
    own_ref, other_ref = outs[:2]
    grad_refs = outs[2 : 2 + X_SIZE]
    rows_ref, grad_ref, w_ref = outs[-3:]
    *token_refs, arrived_ref = token_refs
    step = pl.program_id(0)
    last = place_ref[X_SIZE * CORES] * (TOKEN_STEPS) + first + step == CORES * TOKEN_STEPS - 1
    q_blocks, g_blocks = [], []
    for which, blocks in enumerate((q_blocks, g_blocks)):
        rows, following, their_rows, their_following = token_refs[4 * which : 4 * which + 4]
        blocks.append(shifted(rows[...], jnp.where(last, arrived_ref[which], following[...])))
        blocks.append(shifted(their_rows[0], their_following[0]))
    entries, part_rows = pieces[0].shape[1:3]
    nbr = X_SIZE * CORES * part_rows
    width = heads * HEAD_DIM
    scale = 1.0 / math.sqrt(HEAD_DIM)

    @pl.when(step == 0)
    def _():
        for i, ref in enumerate(w_refs):
            w_ref[:, i * width : (i + 1) * width] = ref[...]

    where = [(across, core) for across in range(X_SIZE) for core in range(CORES)]
    for across, core in where:
        start = pl.multiple_of(place_ref[across * CORES + core] * part_rows, part_rows)
        for e in range(entries):
            rows_ref[e, pl.ds(start, part_rows), :] = pieces[across][core, e]
    blocks = entries // 2
    rows = rows_ref[...].reshape(entries * nbr, -1)
    both = nn(rows, w_ref[...]).astype(jnp.bfloat16)
    jobs = [(b, c, h) for b in range(blocks) for c in range(CORES) for h in range(heads)]
    count = range(len(jobs))
    token = [slice(b * BLOCK_LEN, (b + 1) * BLOCK_LEN) for b, _, _ in jobs]
    cols = [slice(h * HEAD_DIM, (h + 1) * HEAD_DIM) for _, _, h in jobs]
    keys = [slice(b * 2 * nbr, (b + 1) * 2 * nbr) for b, _, _ in jobs]
    base = [2 * c * width + h * HEAD_DIM for _, c, h in jobs]
    q = [q_blocks[jobs[i][1]][token[i], cols[i]] for i in count]
    g = [g_blocks[jobs[i][1]][token[i], cols[i]] for i in count]
    k = [both[keys[i], base[i] : base[i] + HEAD_DIM] for i in count]
    v = [both[keys[i], width + base[i] : width + base[i] + HEAD_DIM] for i in count]
    scores = [nt(q[i], k[i]) for i in count]
    slope = [nt(g[i], v[i]) for i in count]
    raised = [jnp.exp(scores[i] * scale) for i in count]
    inverse = [1.0 / jnp.sum(raised[i], axis=-1, keepdims=True) for i in count]
    probs = [raised[i] * inverse[i] for i in count]
    rounded = [probs[i].astype(jnp.bfloat16) for i in count]
    delta = [jnp.sum(probs[i] * slope[i], axis=-1, keepdims=True) for i in count]
    shaped = [(probs[i] * (slope[i] - delta[i])).astype(jnp.bfloat16) for i in count]
    for i in count:
        result = (own_ref, other_ref)[jobs[i][1]]
        result[0, token[i], cols[i]] = nn(rounded[i], v[i]).astype(jnp.bfloat16)
        result[1, token[i], cols[i]] = (nn(shaped[i], k[i]) * scale).astype(jnp.bfloat16)
    dk = [(tn(q[i], shaped[i]) * scale).astype(jnp.bfloat16) for i in count]
    dv = [tn(g[i], rounded[i]).astype(jnp.bfloat16) for i in count]
    columns = []
    for b in range(blocks):
        terms = []
        for c in range(CORES):
            at = (b * CORES + c) * heads
            terms += dk[at : at + heads] + dv[at : at + heads]
        columns.append(jnp.concatenate(terms, axis=0))
    grad_ref[...] = nn(w_ref[...], jnp.concatenate(columns, axis=1)).astype(jnp.bfloat16)
    for across, core in where:
        start = pl.multiple_of(place_ref[across * CORES + core] * share, 16)
        terms = grad_ref[pl.ds(start, share), :]
        for e in range(entries):
            grad_refs[across][core, e] = terms[:, e * nbr : (e + 1) * nbr]


def attention(peers, tokens, others, arrived, weights, pieces, group, share):
    features = tokens[0].shape[1]
    heads = features // HEAD_DIM
    _, entries, part_rows, encoder = pieces[0].shape
    nbr = X_SIZE * CORES * part_rows
    blocks = entries // 2
    steps = blocks // STEP_BLOCKS
    token_rows = STEP_BLOCKS * BLOCK_LEN
    first = group * steps
    step_entries = 2 * STEP_BLOCKS
    end = tokens[0].shape[0] // BLOCK_LEN - 1

    def own_rows(i, s):
        return s[X_SIZE * CORES] * TOKEN_STEPS + first + i, 0

    def own_following(i, s):
        return jnp.minimum((s[X_SIZE * CORES] * TOKEN_STEPS + first + i + 1) * STEP_BLOCKS, end), 0

    in_specs = []
    for which in range(2):
        in_specs += [
            pl.BlockSpec((token_rows, features), own_rows),
            pl.BlockSpec((BLOCK_LEN, features), own_following),
            pl.BlockSpec((1, token_rows, features), lambda i, s, which=which: (which, first + i, 0)),
            pl.BlockSpec((1, BLOCK_LEN, features), lambda i, s, which=which: (which, (first + i + 1) * STEP_BLOCKS, 0)),
        ]
    in_specs.append(pl.BlockSpec(arrived.shape, lambda i, s: (0, 0, 0)))
    in_specs += [pl.BlockSpec(weight.shape, lambda i, s: (0, 0)) for weight in weights]
    in_specs += [
        pl.BlockSpec((CORES, step_entries) + piece.shape[2:], lambda i, s: (0, i, 0, 0)) for piece in pieces
    ]
    out_shape = [jax.ShapeDtypeStruct((2, blocks * BLOCK_LEN, features), jnp.bfloat16)] * CORES
    out_specs = [pl.BlockSpec((2, token_rows, features), lambda i, s: (0, i, 0))] * CORES
    for piece in pieces:
        out_shape.append(jax.ShapeDtypeStruct((piece.shape[0], entries, share, nbr), jnp.bfloat16))
        out_specs.append(pl.BlockSpec((piece.shape[0], step_entries, share, nbr), lambda i, s: (0, i, 0, 0)))
    flops = blocks * 2 * (2 * 2 * nbr * encoder * 2 * CORES * features + 6 * BLOCK_LEN * 2 * nbr * CORES * features)
    moved = 2 * 2 * entries * nbr * encoder + 4 * CORES * weights[0].size
    return pl.pallas_call(
        functools.partial(attention_kernel, heads=heads, share=share, first=first),
        out_shape=out_shape,
        grid_spec=pltpu.PrefetchScalarGridSpec(
            num_scalar_prefetch=1,
            grid=(steps,),
            in_specs=in_specs,
            out_specs=out_specs,
            scratch_shapes=[
                pltpu.VMEM((step_entries, nbr, encoder), jnp.bfloat16),
                pltpu.VMEM((encoder, step_entries * nbr), jnp.bfloat16),
                pltpu.VMEM((encoder, 2 * CORES * features), jnp.bfloat16),
            ],
        ),
        compiler_params=pltpu.CompilerParams(vmem_limit_bytes=VMEM_LIMIT),
        cost_estimate=pl.CostEstimate(flops=2 * flops, bytes_accessed=moved, transcendentals=0),
        name="attend",
    )(
        peers,
        *[array for own in tokens for array in (own, own, others, others)],
        arrived,
        *weights,
        *pieces,
    )


def gather_near(own):
    return {d: receive_z(own, d) if d else own for d in NEAR_Z}


def gather_lines(got):
    got = dict(got)
    near = jnp.concatenate([got[d] for d in NEAR_Z], axis=0)
    got[3], got[4], got[5] = receive_z(got[2], 1), receive_z(got[0], 4), receive_z(got[6], -1)
    near_up, near_down = receive_y(near, 1), receive_y(near, -1)
    near_up, near_down, *got = lax.optimization_barrier((near_up, near_down, got[3], got[4], got[5]))
    far = jnp.concatenate(got, axis=0)
    middle = near.shape[0] // 2
    near_halves = [receive_y(near_up[:middle], 1), receive_y(near_down[middle:], -1)]
    far_up, far_down = receive_y(far, 1), receive_y(far, -1)
    near_halves, far_up, far_down = lax.optimization_barrier((near_halves, far_up, far_down))
    middle = far.shape[0] // 2
    far_halves = [receive_y(far_up[:middle], 1), receive_y(far_down[middle:], -1)]
    return [near, near_up, near_down] + near_halves + [far, far_up, far_down] + far_halves


def ring_scatter(near, first, second, receive, size):
    half = size // 2
    middle = first.shape[0]
    up, down = receive(first, -1), receive(second, 1)
    for distance in range(half - 1, 0, -1):
        ahead, behind = near[distance], near[size - distance]
        if distance == half - 1:
            ahead = jnp.concatenate([add(ahead[:middle], up), ahead[middle:]])
            behind = jnp.concatenate([behind[:middle], add(behind[middle:], down)])
        else:
            ahead, behind = add(ahead, up), add(behind, down)
        up, down = receive(ahead, -1), receive(behind, 1)
    return add(near[0], up, down)


def scatter_lines(tables):
    near, far = [], []
    for line, part in ((far, tables[Y_SIZE + 1 :]), (near, tables[: Y_SIZE + 1])):
        distances = [d for d in range(Y_SIZE) if d != Y_SIZE // 2]
        line.append(ring_scatter(dict(zip(distances, part[:-2])), *part[-2:], receive_y, Y_SIZE))
    term = {}
    for line, distances in ((near[0], NEAR_Z), (far[0], FAR_Z)):
        entries = line.shape[0] // len(distances)
        for i, d in enumerate(distances):
            term[d] = line[i * entries : (i + 1) * entries]
    ahead, fourth, behind = receive_z(term[3], -1), receive_z(term[4], -4), receive_z(term[5], 1)
    ahead, behind = add(term[2], ahead), add(term[6], behind)
    total = add(
        term[0],
        receive_z(term[1], -1),
        receive_z(term[7], 1),
        receive_z(ahead, -2),
        receive_z(behind, 2),
        fourth,
    )
    return total, near[0]


def gather_whole(own, earlier):
    line = jnp.concatenate(straight_gather(own, receive_y, Y_SIZE), axis=0)
    line = after(line, earlier)
    return [lax.all_gather(line, "z", axis=0, tiled=True)]


def scatter_whole(tables):
    line = lax.psum_scatter(tables[0], "z", scatter_dimension=0, tiled=True)
    entries = line.shape[0] // Y_SIZE
    terms = [line[d * entries : (d + 1) * entries] for d in range(Y_SIZE)]
    return straight_scatter(terms, receive_y, Y_SIZE)


def table_sizes(entries):
    lines = []
    for line in (NEAR_Z, FAR_Z):
        rows = len(line) * entries
        lines += [rows] * (Y_SIZE - 1) + [rows // 2] * 2
    return lines, [Z_SIZE * Y_SIZE * entries]


def shards(queries, cotangent, neighbours, key_weight, value_weight, retrieval):
    token_rows, features = queries.shape
    entries, nbr, encoder = neighbours.shape
    peers_count = X_SIZE * CORES
    z, y, x, core = (lax.axis_index(axis) for axis in ("z", "y", "x", "core"))
    tensor_index = x * CORES + core
    offset_rows = BLOCK_LEN - 1
    sequence_devices = SEQ_LEN // token_rows
    seq_axes, seq_size = ("z", "y"), Z_SIZE * Y_SIZE
    inside = [(i, i + 1) for i in range(seq_size) if (i + 1) % sequence_devices]

    part_rows, share = nbr // peers_count, encoder // peers_count
    mine = lax.dynamic_slice_in_dim(neighbours, tensor_index * part_rows, part_rows, axis=1)
    cut = [mine[:, :, lo : lo + width] for lo, width in PARTS]
    away_weights = [other_core(key_weight), other_core(value_weight)]
    weights = [key_weight, value_weight] + away_weights
    cut[0] = after(cut[0], away_weights)
    near = gather_near(cut[0])
    parts = [gather_lines(near), gather_whole(cut[1], [near[d] for d in NEAR_Z if d])]

    leading = jnp.stack([queries[:BLOCK_LEN], cotangent[:BLOCK_LEN]])
    arrived = lax.ppermute(leading, seq_axes, [(b, a) for a, b in inside])

    core_rows = token_rows // CORES
    away = (1 - core) * core_rows
    inner = jnp.stack([array[core_rows : core_rows + BLOCK_LEN] for array in (queries, cotangent)])
    others = other_core(
        jnp.concatenate(
            [
                jnp.stack([lax.dynamic_slice_in_dim(array, away, core_rows) for array in (queries, cotangent)]),
                jnp.where(core == 1, inner, arrived),
            ],
            axis=1,
        )
    )
    peers = jnp.stack(
        [((x + dx) % X_SIZE) * CORES + (core + dc) % CORES for dx in range(X_SIZE) for dc in range(CORES)] + [core]
    ).astype(jnp.int32)

    kept, sent = pick(parts[0] + parts[1], retrieval)
    came = other_core(sent)
    group_entries = kept.shape[0] // GROUPS

    results, summed, pieces = [], [], None
    both = jnp.stack([kept, came])
    for group in range(GROUPS):
        held = both[:, group * group_entries : (group + 1) * group_entries]
        if pieces is not None:
            held = after(held, pieces[1:])
        pieces = straight_gather(held, receive_x, X_SIZE)
        own, other, *grads = attention(
            peers, (queries, cotangent), others, arrived, weights, pieces, group, share
        )
        results.append((own, other))
        summed.append(straight_scatter(grads, receive_x, X_SIZE))

    own, other = (jnp.concatenate(pair, axis=1) for pair in zip(*results))
    back = other_core(other)
    extended = jnp.where(core == 0, jnp.concatenate([own, back], axis=1), jnp.concatenate([back, own], axis=1))
    carried = lax.ppermute(extended[:, token_rows - offset_rows :], seq_axes, inside)
    summed = jnp.concatenate(summed, axis=1)
    tables = place([summed[0], other_core(summed[1])], retrieval)
    share, near = scatter_lines(tables[:-1])
    shares = [share, scatter_whole(tables[-1:])]
    carried = after(carried, near)
    settled = [
        jnp.concatenate([carried[which], extended[which, : token_rows - offset_rows]], axis=0) for which in range(2)
    ]
    neighbour_grad = jnp.concatenate(shares, axis=1).transpose(0, 2, 1)
    return settled[0], settled[1], neighbour_grad


def solution(mesh):
    axes = Mesh(mesh.devices.reshape(Z_SIZE, Y_SIZE, X_SIZE, CORES), ("z", "y", "x", "core"))
    seq, tensor = ("z", "y"), ("x", "core")
    placed = (
        P(seq, tensor),
        P(seq, tensor),
        P(seq, None, None),
        P(None, tensor),
        P(None, tensor),
        P(seq, None),
    )
    return jax.shard_map(
        shards,
        mesh=axes,
        in_specs=placed,
        out_specs=(P(seq, tensor), P(seq, tensor), P(seq, None, tensor)),
        check_vma=False,
    )
```

```python
import functools
import math

import jax
import jax.numpy as jnp
from jax import lax
from jax.experimental import pallas as pl
from jax.experimental.pallas import tpu as pltpu
from jax.sharding import Mesh
from jax.sharding import PartitionSpec as P

HEAD_DIM = 128
BLOCK_LEN = 64
SEQ_LEN = 2048
Z_SIZE, Y_SIZE, X_SIZE, CORES = 8, 4, 4, 2
PARTS = ((0, 512), (512, 384))
GRAD_PARTS = ((0, 64), (64, 48))
NEAR_Z, FAR_Z = (0, 1, 2, 6, 7), (3, 4, 5)
GROUPS = 2
ENTRIES_DEV = 8
STEP_BLOCKS = 4
TOKEN_STEPS = 2
VMEM_LIMIT = 56 * 1024 * 1024


def receive_on(axis, size):
    def receive(block, k):
        return lax.ppermute(block, axis, [((i + k) % size, i) for i in range(size)])

    return receive


receive_z = receive_on("z", Z_SIZE)
receive_y = receive_on("y", Y_SIZE)
receive_x = receive_on("x", X_SIZE)
other_core = functools.partial(receive_on("core", CORES), k=1)


def after(blocks, earlier):
    return lax.optimization_barrier((blocks, earlier))[0]


def straight_gather(own, receive, size):
    return [own] + [receive(own, k) for k in range(1, size)]


def straight_scatter(terms, receive, size):
    return add(terms[0], *[receive(terms[k], -k) for k in range(1, size)])


def add(*terms):
    total = terms[0].astype(jnp.float32)
    for term in terms[1:]:
        total = total + term.astype(jnp.float32)
    return total.astype(jnp.bfloat16)


def used_entry(pairs_ref, i, count):
    core = lax.axis_index("core")
    half = count // CORES
    turned = lax.rem(core * half + i, count)
    entry = pairs_ref[turned // 2, lax.rem(turned, 2)]
    holder, local = entry // ENTRIES_DEV, lax.rem(entry, ENTRIES_DEV)
    z, y = holder // Y_SIZE, lax.rem(holder, Y_SIZE)
    far_z = lax.rem(z + Z_SIZE - lax.axis_index("z"), Z_SIZE)
    far_y = lax.rem(y + Y_SIZE - lax.axis_index("y"), Y_SIZE)
    return z, far_z, far_y, local


def line_spot(far_z, far_y, local):
    line = jnp.int32(0)
    place = jnp.int32(0)
    for which, distances in enumerate((NEAR_Z, FAR_Z)):
        for i, d in enumerate(distances):
            line = jnp.where(far_z == d, which, line)
            place = jnp.where(far_z == d, i, place)
    row, half = place * ENTRIES_DEV + local, Y_SIZE // 2
    middle = jnp.where(line == 1, len(FAR_Z), len(NEAR_Z)) * ENTRIES_DEV // 2
    late = jnp.logical_and(far_y == half, row >= middle)
    table = jnp.where(far_y < half, far_y, far_y - 1)
    table = jnp.where(far_y == half, jnp.where(late, Y_SIZE, Y_SIZE - 1), table)
    return line, table, jnp.where(late, row - middle, row)


def at_spots(pairs_ref, i, count, tables, act):
    z, far_z, far_y, local = used_entry(pairs_ref, i, count)
    line, table, row = line_spot(far_z, far_y, local)
    for which in range(2):

        @pl.when(line == which)
        def _():
            for k in range(Y_SIZE + 1):

                @pl.when(table == k)
                def _(held=tables[which * (Y_SIZE + 1) + k]):
                    act(0, held, row)

    act(1, tables[-1], (z * Y_SIZE + far_y) * ENTRIES_DEV + local)


def pick_kernel(count, pairs_ref, *refs):
    tables, outs = refs[:-CORES], refs[-CORES:]
    starts = [lo for lo, _ in PARTS]

    def one(i, carry, picked, first):
        def act(part, held, row):
            lo = starts[part]
            picked[i, :, lo : lo + held.shape[2]] = held[row]

        at_spots(pairs_ref, first + i, count, tables, act)
        return carry

    half = count // CORES
    for core in range(CORES):
        lax.fori_loop(0, half, functools.partial(one, picked=outs[core], first=core * half), 0)


def pick(tables, pairs):
    count = pairs.size
    width = sum(width for _, width in PARTS)
    shape = jax.ShapeDtypeStruct((count // CORES, tables[0].shape[1], width), jnp.bfloat16)
    return pl.pallas_call(
        functools.partial(pick_kernel, count),
        out_shape=[shape] * CORES,
        in_specs=[pl.BlockSpec(memory_space=pltpu.SMEM)] + [pl.BlockSpec(memory_space=pltpu.VMEM)] * len(tables),
        out_specs=[pl.BlockSpec(memory_space=pltpu.VMEM)] * CORES,
        compiler_params=pltpu.CompilerParams(vmem_limit_bytes=VMEM_LIMIT),
        name="pick",
    )(pairs, *tables)


def place_kernel(count, pairs_ref, *refs):
    given, tables = refs[:CORES], refs[CORES:]
    for table in tables:
        table[...] = jnp.zeros(table.shape, table.dtype)
    starts = [lo for lo, _ in GRAD_PARTS]

    def one(i, carry, terms, first):
        def act(part, held, row):
            lo = starts[part]
            term = terms[i, lo : lo + held.shape[1]].astype(jnp.float32)
            held[row] = (held[row].astype(jnp.float32) + term).astype(held.dtype)

        at_spots(pairs_ref, first + i, count, tables, act)
        return carry

    half = count // CORES
    for core in range(CORES):
        lax.fori_loop(0, half, functools.partial(one, terms=given[core], first=core * half), 0)


def place(given, pairs):
    nbr = given[0].shape[2]
    shapes = [
        jax.ShapeDtypeStruct((size, width, nbr), jnp.bfloat16)
        for (_, width), sizes in zip(GRAD_PARTS, table_sizes(ENTRIES_DEV))
        for size in sizes
    ]
    return pl.pallas_call(
        functools.partial(place_kernel, pairs.size),
        out_shape=shapes,
        in_specs=[pl.BlockSpec(memory_space=pltpu.SMEM)] + [pl.BlockSpec(memory_space=pltpu.VMEM)] * len(given),
        out_specs=[pl.BlockSpec(memory_space=pltpu.VMEM)] * len(shapes),
        compiler_params=pltpu.CompilerParams(vmem_limit_bytes=VMEM_LIMIT),
        name="place",
    )(pairs, *given)


def nt(a, b):
    return lax.dot_general(a, b, (((1,), (1,)), ((), ())), preferred_element_type=jnp.float32)


def tn(a, b):
    return lax.dot_general(a, b, (((0,), (0,)), ((), ())), preferred_element_type=jnp.float32)


def nn(a, b):
    return jnp.dot(a, b, preferred_element_type=jnp.float32)


def shifted(rows, following):
    rows = jnp.concatenate([rows.astype(jnp.float32), following.astype(jnp.float32)], axis=0)
    count = rows.shape[0]
    return pltpu.roll(rows, count - (BLOCK_LEN - 1), 0)[: count - BLOCK_LEN].astype(jnp.bfloat16)


def attention_kernel(place_ref, *refs, heads, share, first):
    token_refs, w_refs, refs = refs[:9], refs[9 : 9 + 2 * CORES], refs[9 + 2 * CORES :]
    pieces, outs = refs[:X_SIZE], refs[X_SIZE:]
    own_ref, other_ref = outs[:2]
    grad_refs = outs[2 : 2 + X_SIZE]
    rows_ref, grad_ref, w_ref = outs[-3:]
    *token_refs, arrived_ref = token_refs
    step = pl.program_id(0)
    last = place_ref[X_SIZE * CORES] * (TOKEN_STEPS) + first + step == CORES * TOKEN_STEPS - 1
    q_blocks, g_blocks = [], []
    for which, blocks in enumerate((q_blocks, g_blocks)):
        rows, following, their_rows, their_following = token_refs[4 * which : 4 * which + 4]
        blocks.append(shifted(rows[...], jnp.where(last, arrived_ref[which], following[...])))
        blocks.append(shifted(their_rows[0], their_following[0]))
    entries, part_rows = pieces[0].shape[1:3]
    nbr = X_SIZE * CORES * part_rows
    width = heads * HEAD_DIM
    scale = 1.0 / math.sqrt(HEAD_DIM)

    @pl.when(step == 0)
    def _():
        for i, ref in enumerate(w_refs):
            w_ref[:, i * width : (i + 1) * width] = ref[...]

    where = [(across, core) for across in range(X_SIZE) for core in range(CORES)]
    for across, core in where:
        start = pl.multiple_of(place_ref[across * CORES + core] * part_rows, part_rows)
        for e in range(entries):
            rows_ref[e, pl.ds(start, part_rows), :] = pieces[across][core, e]
    blocks = entries // 2
    rows = rows_ref[...].reshape(entries * nbr, -1)
    both = nn(rows, w_ref[...]).astype(jnp.bfloat16)
    jobs = [(b, c, h) for b in range(blocks) for c in range(CORES) for h in range(heads)]
    count = range(len(jobs))
    token = [slice(b * BLOCK_LEN, (b + 1) * BLOCK_LEN) for b, _, _ in jobs]
    cols = [slice(h * HEAD_DIM, (h + 1) * HEAD_DIM) for _, _, h in jobs]
    keys = [slice(b * 2 * nbr, (b + 1) * 2 * nbr) for b, _, _ in jobs]
    base = [2 * c * width + h * HEAD_DIM for _, c, h in jobs]
    q = [q_blocks[jobs[i][1]][token[i], cols[i]] for i in count]
    g = [g_blocks[jobs[i][1]][token[i], cols[i]] for i in count]
    k = [both[keys[i], base[i] : base[i] + HEAD_DIM] for i in count]
    v = [both[keys[i], width + base[i] : width + base[i] + HEAD_DIM] for i in count]
    scores = [nt(q[i], k[i]) for i in count]
    slope = [nt(g[i], v[i]) for i in count]
    raised = [jnp.exp(scores[i] * scale) for i in count]
    inverse = [1.0 / jnp.sum(raised[i], axis=-1, keepdims=True) for i in count]
    probs = [raised[i] * inverse[i] for i in count]
    rounded = [probs[i].astype(jnp.bfloat16) for i in count]
    delta = [jnp.sum(probs[i] * slope[i], axis=-1, keepdims=True) for i in count]
    shaped = [(probs[i] * (slope[i] - delta[i])).astype(jnp.bfloat16) for i in count]
    for i in count:
        result = (own_ref, other_ref)[jobs[i][1]]
        result[0, token[i], cols[i]] = nn(rounded[i], v[i]).astype(jnp.bfloat16)
        result[1, token[i], cols[i]] = (nn(shaped[i], k[i]) * scale).astype(jnp.bfloat16)
    dk = [(tn(q[i], shaped[i]) * scale).astype(jnp.bfloat16) for i in count]
    dv = [tn(g[i], rounded[i]).astype(jnp.bfloat16) for i in count]
    columns = []
    for b in range(blocks):
        terms = []
        for c in range(CORES):
            at = (b * CORES + c) * heads
            terms += dk[at : at + heads] + dv[at : at + heads]
        columns.append(jnp.concatenate(terms, axis=0))
    grad_ref[...] = nn(w_ref[...], jnp.concatenate(columns, axis=1)).astype(jnp.bfloat16)
    for across, core in where:
        start = pl.multiple_of(place_ref[across * CORES + core] * share, 16)
        terms = grad_ref[pl.ds(start, share), :]
        for e in range(entries):
            grad_refs[across][core, e] = terms[:, e * nbr : (e + 1) * nbr]


def attention(peers, tokens, others, arrived, weights, pieces, group, share):
    features = tokens[0].shape[1]
    heads = features // HEAD_DIM
    _, entries, part_rows, encoder = pieces[0].shape
    nbr = X_SIZE * CORES * part_rows
    blocks = entries // 2
    steps = blocks // STEP_BLOCKS
    token_rows = STEP_BLOCKS * BLOCK_LEN
    first = group * steps
    step_entries = 2 * STEP_BLOCKS
    end = tokens[0].shape[0] // BLOCK_LEN - 1

    def own_rows(i, s):
        return s[X_SIZE * CORES] * TOKEN_STEPS + first + i, 0

    def own_following(i, s):
        return jnp.minimum((s[X_SIZE * CORES] * TOKEN_STEPS + first + i + 1) * STEP_BLOCKS, end), 0

    in_specs = []
    for which in range(2):
        in_specs += [
            pl.BlockSpec((token_rows, features), own_rows),
            pl.BlockSpec((BLOCK_LEN, features), own_following),
            pl.BlockSpec((1, token_rows, features), lambda i, s, which=which: (which, first + i, 0)),
            pl.BlockSpec((1, BLOCK_LEN, features), lambda i, s, which=which: (which, (first + i + 1) * STEP_BLOCKS, 0)),
        ]
    in_specs.append(pl.BlockSpec(arrived.shape, lambda i, s: (0, 0, 0)))
    in_specs += [pl.BlockSpec(weight.shape, lambda i, s: (0, 0)) for weight in weights]
    in_specs += [
        pl.BlockSpec((CORES, step_entries) + piece.shape[2:], lambda i, s: (0, i, 0, 0)) for piece in pieces
    ]
    out_shape = [jax.ShapeDtypeStruct((2, blocks * BLOCK_LEN, features), jnp.bfloat16)] * CORES
    out_specs = [pl.BlockSpec((2, token_rows, features), lambda i, s: (0, i, 0))] * CORES
    for piece in pieces:
        out_shape.append(jax.ShapeDtypeStruct((piece.shape[0], entries, share, nbr), jnp.bfloat16))
        out_specs.append(pl.BlockSpec((piece.shape[0], step_entries, share, nbr), lambda i, s: (0, i, 0, 0)))
    flops = blocks * 2 * (2 * 2 * nbr * encoder * 2 * CORES * features + 6 * BLOCK_LEN * 2 * nbr * CORES * features)
    moved = 2 * 2 * entries * nbr * encoder + 4 * CORES * weights[0].size
    return pl.pallas_call(
        functools.partial(attention_kernel, heads=heads, share=share, first=first),
        out_shape=out_shape,
        grid_spec=pltpu.PrefetchScalarGridSpec(
            num_scalar_prefetch=1,
            grid=(steps,),
            in_specs=in_specs,
            out_specs=out_specs,
            scratch_shapes=[
                pltpu.VMEM((step_entries, nbr, encoder), jnp.bfloat16),
                pltpu.VMEM((encoder, step_entries * nbr), jnp.bfloat16),
                pltpu.VMEM((encoder, 2 * CORES * features), jnp.bfloat16),
            ],
        ),
        compiler_params=pltpu.CompilerParams(vmem_limit_bytes=VMEM_LIMIT),
        cost_estimate=pl.CostEstimate(flops=2 * flops, bytes_accessed=moved, transcendentals=0),
        name="attend",
    )(
        peers,
        *[array for own in tokens for array in (own, own, others, others)],
        arrived,
        *weights,
        *pieces,
    )


def gather_near(own):
    return {d: receive_z(own, d) if d else own for d in NEAR_Z}


def gather_lines(got):
    got = dict(got)
    near = jnp.concatenate([got[d] for d in NEAR_Z], axis=0)
    got[3], got[4], got[5] = receive_z(got[2], 1), receive_z(got[0], 4), receive_z(got[6], -1)
    near_up, near_down = receive_y(near, 1), receive_y(near, -1)
    near_up, near_down, *got = lax.optimization_barrier((near_up, near_down, got[3], got[4], got[5]))
    far = jnp.concatenate(got, axis=0)
    middle = near.shape[0] // 2
    near_halves = [receive_y(near_up[:middle], 1), receive_y(near_down[middle:], -1)]
    far_up, far_down = receive_y(far, 1), receive_y(far, -1)
    near_halves, far_up, far_down = lax.optimization_barrier((near_halves, far_up, far_down))
    middle = far.shape[0] // 2
    far_halves = [receive_y(far_up[:middle], 1), receive_y(far_down[middle:], -1)]
    return [near, near_up, near_down] + near_halves + [far, far_up, far_down] + far_halves


def ring_scatter(near, first, second, receive, size):
    half = size // 2
    middle = first.shape[0]
    up, down = receive(first, -1), receive(second, 1)
    for distance in range(half - 1, 0, -1):
        ahead, behind = near[distance], near[size - distance]
        if distance == half - 1:
            ahead = jnp.concatenate([add(ahead[:middle], up), ahead[middle:]])
            behind = jnp.concatenate([behind[:middle], add(behind[middle:], down)])
        else:
            ahead, behind = add(ahead, up), add(behind, down)
        up, down = receive(ahead, -1), receive(behind, 1)
    return add(near[0], up, down)


def scatter_lines(tables):
    near, far = [], []
    for line, part in ((far, tables[Y_SIZE + 1 :]), (near, tables[: Y_SIZE + 1])):
        distances = [d for d in range(Y_SIZE) if d != Y_SIZE // 2]
        line.append(ring_scatter(dict(zip(distances, part[:-2])), *part[-2:], receive_y, Y_SIZE))
    term = {}
    for line, distances in ((near[0], NEAR_Z), (far[0], FAR_Z)):
        entries = line.shape[0] // len(distances)
        for i, d in enumerate(distances):
            term[d] = line[i * entries : (i + 1) * entries]
    ahead, fourth, behind = receive_z(term[3], -1), receive_z(term[4], -4), receive_z(term[5], 1)
    ahead, behind = add(term[2], ahead), add(term[6], behind)
    total = add(
        term[0],
        receive_z(term[1], -1),
        receive_z(term[7], 1),
        receive_z(ahead, -2),
        receive_z(behind, 2),
        fourth,
    )
    return total, near[0]


def gather_whole(own, earlier):
    line = jnp.concatenate(straight_gather(own, receive_y, Y_SIZE), axis=0)
    line = after(line, earlier)
    return [lax.all_gather(line, "z", axis=0, tiled=True)]


def scatter_whole(tables):
    line = lax.psum_scatter(tables[0], "z", scatter_dimension=0, tiled=True)
    entries = line.shape[0] // Y_SIZE
    terms = [line[d * entries : (d + 1) * entries] for d in range(Y_SIZE)]
    return straight_scatter(terms, receive_y, Y_SIZE)


def table_sizes(entries):
    lines = []
    for line in (NEAR_Z, FAR_Z):
        rows = len(line) * entries
        lines += [rows] * (Y_SIZE - 1) + [rows // 2] * 2
    return lines, [Z_SIZE * Y_SIZE * entries]


def shards(queries, cotangent, neighbours, key_weight, value_weight, retrieval):
    token_rows, features = queries.shape
    entries, nbr, encoder = neighbours.shape
    peers_count = X_SIZE * CORES
    z, y, x, core = (lax.axis_index(axis) for axis in ("z", "y", "x", "core"))
    tensor_index = x * CORES + core
    offset_rows = BLOCK_LEN - 1
    sequence_devices = SEQ_LEN // token_rows
    seq_axes, seq_size = ("z", "y"), Z_SIZE * Y_SIZE
    inside = [(i, i + 1) for i in range(seq_size) if (i + 1) % sequence_devices]

    part_rows, share = nbr // peers_count, encoder // peers_count
    mine = lax.dynamic_slice_in_dim(neighbours, tensor_index * part_rows, part_rows, axis=1)
    cut = [mine[:, :, lo : lo + width] for lo, width in PARTS]
    away_weights = [other_core(key_weight), other_core(value_weight)]
    weights = [key_weight, value_weight] + away_weights
    cut[0] = after(cut[0], away_weights)
    near = gather_near(cut[0])
    parts = [gather_lines(near), gather_whole(cut[1], [near[d] for d in NEAR_Z if d])]

    leading = jnp.stack([queries[:BLOCK_LEN], cotangent[:BLOCK_LEN]])
    arrived = lax.ppermute(leading, seq_axes, [(b, a) for a, b in inside])

    core_rows = token_rows // CORES
    away = (1 - core) * core_rows
    inner = jnp.stack([array[core_rows : core_rows + BLOCK_LEN] for array in (queries, cotangent)])
    others = other_core(
        jnp.concatenate(
            [
                jnp.stack([lax.dynamic_slice_in_dim(array, away, core_rows) for array in (queries, cotangent)]),
                jnp.where(core == 1, inner, arrived),
            ],
            axis=1,
        )
    )
    peers = jnp.stack(
        [((x + dx) % X_SIZE) * CORES + (core + dc) % CORES for dx in range(X_SIZE) for dc in range(CORES)] + [core]
    ).astype(jnp.int32)

    kept, sent = pick(parts[0] + parts[1], retrieval)
    came = other_core(sent)
    group_entries = kept.shape[0] // GROUPS

    results, summed, pieces = [], [], None
    both = jnp.stack([kept, came])
    for group in range(GROUPS):
        held = both[:, group * group_entries : (group + 1) * group_entries]
        if pieces is not None:
            held = after(held, pieces[1:])
        pieces = straight_gather(held, receive_x, X_SIZE)
        own, other, *grads = attention(
            peers, (queries, cotangent), others, arrived, weights, pieces, group, share
        )
        results.append((own, other))
        summed.append(straight_scatter(grads, receive_x, X_SIZE))

    own, other = (jnp.concatenate(pair, axis=1) for pair in zip(*results))
    back = other_core(other)
    extended = jnp.where(core == 0, jnp.concatenate([own, back], axis=1), jnp.concatenate([back, own], axis=1))
    carried = lax.ppermute(extended[:, token_rows - offset_rows :], seq_axes, inside)
    summed = jnp.concatenate(summed, axis=1)
    tables = place([summed[0], other_core(summed[1])], retrieval)
    share, near = scatter_lines(tables[:-1])
    shares = [share, scatter_whole(tables[-1:])]
    carried = after(carried, near)
    settled = [
        jnp.concatenate([carried[which], extended[which, : token_rows - offset_rows]], axis=0) for which in range(2)
    ]
    neighbour_grad = jnp.concatenate(shares, axis=1).transpose(0, 2, 1)
    return settled[0], settled[1], neighbour_grad


def solution(mesh):
    axes = Mesh(mesh.devices.reshape(Z_SIZE, Y_SIZE, X_SIZE, CORES), ("z", "y", "x", "core"))
    seq, tensor = ("z", "y"), ("x", "core")
    placed = (
        P(seq, tensor),
        P(seq, tensor),
        P(seq, None, None),
        P(None, tensor),
        P(None, tensor),
        P(seq, None),
    )
    return jax.shard_map(
        shards,
        mesh=axes,
        in_specs=placed,
        out_specs=(P(seq, tensor), P(seq, tensor), P(seq, None, tensor)),
        check_vma=False,
    )
```
